32 devices in a mesh: dp: 4 (over y, x), seq: 8 (over z, core).
Axes of the slice: x: 2, y: 2, z: 4, core: 2. Of those that a mesh axis runs over, the one named last changes fastest.
Arguments:
- loaded: float32 [8, 24, 1664], P('seq', 'dp'), may hold values from -24 to 24
- tile_rows: int32 [8, 24], P('seq', 'dp'), may hold values from 0 to 23, as said below
- bucket_ids: int32 [2], replicated, may hold values from 0 to 3, as said below
- in_weight: float32 [96, 81], replicated, may hold values from -0.625 to 0.625
- in_bias: float32 [96], replicated, may hold values from -3 to 3
- bucket_bias: float32 [4, 96], replicated, may hold values from -4 to 4
- norm_gain: float32 [96], replicated, may hold values from 0.5 to 1.5
- mid_weight: float32 [27, 96, 96], replicated, may hold values from -0.125 to 0.125
- mid_bias: float32 [96], replicated, may hold values from -3 to 3
- head_gain: float32 [96], replicated, may hold values from 0.5 to 1.5
- head_weight: float32 [16, 96], replicated, may hold values from -0.625 to 0.625
- head_bias: float32 [16], replicated, may hold values from -3 to 3
Outputs:
- latent_tokens: float32 [8, 8, 26624], P(None, 'dp', 'seq')
The draws below stay inside these ranges and needn't reach their ends.
Inputs may be any that keep to these rules, and one draw needn't show every extreme that they name: For each frame, tile_rows[g] is a permutation of the 24 tiles. The 6 entries held by one index of dp name at most 2 tiles of any one row band (band o holds tiles 6 * o to 6 * o + 5), and in every frame some index of dp names exactly 2 tiles of some band. `bucket_ids`: clips whose numbers differ by less than 4 have different buckets; clips whose numbers differ by 4 have the same one.
All inputs are finite; a program needn't handle non-finite values.
Results may differ from the reference program's by a relative error of at most 0.0003.
Values sent between devices are 32-bit elements; how exact they have to be, the bound alone decides.
No kernel may reach another device: no remote copies, remote signals or barrier semaphores. Data moves between devices by JAX's collectives and lax.ppermute only.
A program may use at most 128 MiB of HBM per device.

```python
import math
import jax
import jax.numpy as jnp
from jax import lax

CH = 96
ZCH = 16
W = 832
ROWS_DEV = 4
FRAMES = 4
BUCKETS = 4
NF = 8
CLIPS = 2
H = 16
TILES_DEV = 6
TILES_ALL = 24
N_DP = 4


def draw_loaded(key, part):
    key = jax.random.fold_in(key, 11)
    key_unit, key_tile, key_column = jax.random.split(key, 3)
    dims_all = (NF, TILES_ALL, 2 * W)
    unit_values = jnp.clip(jax.random.normal(key_unit, dims_all, jnp.float32), -4.0, 4.0)
    tile_scale = jnp.exp(jax.random.uniform(key_tile, (NF, TILES_ALL, 1), jnp.float32, math.log(0.3), math.log(3.0)))
    column_scale = jnp.exp(jax.random.uniform(key_column, (1, 1, 2 * W), jnp.float32, math.log(0.5), math.log(2.0)))
    return unit_values * tile_scale * column_scale


def draw_tile_rows(key, part):
    key = jax.random.fold_in(key, 23)

    def one_frame(frame_key):
        key_shift, key_owner, key_slot, key_order = jax.random.split(frame_key, 4)
        shifts = jax.random.permutation(key_shift, N_DP)
        owner_perm = jax.random.permutation(key_owner, N_DP)
        slot_perm = jax.random.permutation(key_slot, TILES_DEV)
        loaders = jnp.arange(N_DP, dtype=jnp.int32)[:, None]
        items = jnp.arange(TILES_DEV, dtype=jnp.int32)[None, :]
        classes = items // 2 % N_DP
        owners = owner_perm[(loaders + shifts[classes]) % N_DP]
        position = owners * TILES_DEV + slot_perm[items]
        orders = jax.vmap(lambda order_key: jax.random.permutation(order_key, TILES_DEV))(jax.random.split(key_order, N_DP))
        return jnp.take_along_axis(position, orders, axis=1).reshape(-1)
    return jax.vmap(one_frame)(jax.random.split(key, NF)).astype(jnp.int32)


def draw_bucket_ids(key, part):
    key = jax.random.fold_in(key, 37)
    anchor = jax.random.randint(key, (), 0, min(CLIPS, BUCKETS)).astype(jnp.int32)
    clip_nums = jnp.arange(CLIPS, dtype=jnp.int32)
    return ((BUCKETS - 1 + clip_nums - anchor + BUCKETS * CLIPS) % BUCKETS).astype(jnp.int32)


def bell_draw(stream_key, dims, width, reach, held_as=jnp.bfloat16):
    entries = width * jax.random.normal(stream_key, dims, jnp.float32)
    return jnp.clip(entries, min=-reach, max=reach).astype(held_as)


def setup_inputs(seed: int = 0) -> dict:
    key_list = jax.random.split(jax.random.key(seed), 13)
    loaded = draw_loaded(jax.random.fold_in(key_list[12], 71), 0)
    tile_rows = draw_tile_rows(jax.random.fold_in(key_list[12], 71), 0)
    bucket_ids = draw_bucket_ids(jax.random.fold_in(key_list[12], 71), 0)
    in_weight = bell_draw(key_list[3], (CH, 81), 81 ** -0.5, 0.625, jnp.float32)
    in_bias = bell_draw(key_list[4], (CH,), 0.5, 3.0, jnp.float32)
    bucket_bias = bell_draw(key_list[5], (BUCKETS, CH), 1.0, 4.0, jnp.float32)
    norm_gain = jnp.clip(1.0 + 0.1 * jax.random.normal(key_list[6], (CH,), jnp.float32), 0.5, 1.5)
    mid_weight = bell_draw(key_list[7], (27, CH, CH), (27 * CH) ** -0.5, 0.125, jnp.float32)
    mid_bias = bell_draw(key_list[8], (CH,), 0.5, 3.0, jnp.float32)
    head_gain = jnp.clip(1.0 + 0.1 * jax.random.normal(key_list[9], (CH,), jnp.float32), 0.5, 1.5)
    head_weight = bell_draw(key_list[10], (ZCH, CH), CH ** -0.5, 0.625, jnp.float32)
    head_bias = bell_draw(key_list[11], (ZCH,), 0.5, 3.0, jnp.float32)
    return dict(loaded=loaded, tile_rows=tile_rows, bucket_ids=bucket_ids, in_weight=in_weight, in_bias=in_bias, bucket_bias=bucket_bias, norm_gain=norm_gain, mid_weight=mid_weight, mid_bias=mid_bias, head_gain=head_gain, head_weight=head_weight, head_bias=head_bias)


EPSILON = 1e-06
PRECISE = lax.Precision.HIGHEST

def plane_conv(image, kernel):
    return lax.conv_general_dilated(image[None], kernel, (1, 1), ((1, 1), (1, 1)), dimension_numbers=('NCHW', 'OIHW', 'NCHW'), precision=PRECISE)[0]

def scaled_norm(values, scales):
    square = lax.optimization_barrier(jnp.mean(values * values, axis=0, keepdims=True))
    return values * lax.rsqrt(square + EPSILON) * scales[:, None, None]

def reference(loaded, tile_rows, bucket_ids, in_weight, in_bias, bucket_bias, norm_gain, mid_weight, mid_bias, head_gain, head_weight, head_bias):
    frames_all = loaded.shape[0]
    video = jax.vmap(lambda tile_data, places: jnp.zeros_like(tile_data).at[places].set(tile_data))(loaded, tile_rows)
    video = video.reshape(frames_all, N_DP, 3, ROWS_DEV // 2, 2 * W).transpose(0, 2, 1, 3, 4).reshape(frames_all, 3, H, W)
    video_front = jnp.concatenate([jnp.zeros((4,) + video.shape[1:], jnp.float32), video], 0)
    entry_kernels = in_weight.reshape(CH, 3, 3, 3, 3).transpose(1, 0, 4, 2, 3)
    middle_kernels = mid_weight.reshape(3, 3, 3, CH, CH).transpose(0, 3, 4, 1, 2)

    def first_section(frame_id):
        frame_pos = frame_id % FRAMES
        running = jnp.zeros((CH, H, W), jnp.float32)
        for step_time in range(3):
            where_at = (frame_id - 2 + step_time + 4).astype(jnp.int32)
            source = lax.dynamic_index_in_dim(video_front, where_at, 0, keepdims=False)
            source = jnp.where(frame_pos - 2 + step_time >= 0, source, 0.0)
            running = running + plane_conv(source, entry_kernels[step_time])
        clip_id = (frame_id // FRAMES).astype(jnp.int32)
        bucket_row = bucket_bias[bucket_ids[clip_id]]
        return running + (in_bias + bucket_row)[:, None, None]

    def one_frame(frame_id):
        frame_pos = frame_id % FRAMES
        sections = [first_section(frame_id - 2 + step_time) for step_time in range(3)]
        branch = jnp.zeros((CH, H, W), jnp.float32) + mid_bias[:, None, None]
        for step_time in range(3):
            active = jax.nn.silu(scaled_norm(sections[step_time], norm_gain))
            active = jnp.where(frame_pos - 2 + step_time >= 0, active, 0.0)
            branch = branch + plane_conv(active, middle_kernels[step_time])
        summed = sections[2] + branch
        latent = jax.nn.silu(scaled_norm(summed, head_gain))
        latent = jnp.einsum('zc,chw->zhw', head_weight, latent, precision=PRECISE) + head_bias[:, None, None]
        return latent.reshape(ZCH, H // 2, 2, W // 2, 2).transpose(1, 3, 0, 2, 4).reshape(H // 2, W // 2 * ZCH * 4)
    return lax.map(one_frame, jnp.arange(frames_all, dtype=jnp.int32))
```

```python
import functools

import jax
import jax.numpy as jnp
from jax import lax
from jax.experimental import pallas as pl
from jax.experimental.pallas import tpu as pltpu
from jax.sharding import PartitionSpec as P

FRAMES = 4
EPSILON = 1e-06
LANES = 128
TILES = 6
MOVED = 64
SLOT = 80
BF16 = jnp.bfloat16
F32 = jnp.float32
F8 = jnp.float8_e4m3fn
NT = (((1,), (1,)), ((), ()))
TN = (((0,), (0,)), ((), ()))


def iota(shape, dim):
    return lax.broadcasted_iota(jnp.int32, shape, dim)


def halves(values):
    high = values.astype(BF16)
    return high, (values - high.astype(F32)).astype(BF16)


def mm(a, b):
    return jnp.dot(a, b, preferred_element_type=F32)


def mm_tn(a, b):
    return lax.dot_general(a, b, TN, preferred_element_type=F32)


def send_kernel(groups_dp, groups_seq, row_len, loaded_any, tiles_any, out_ref, loaded_ref, tiles_ref, sems):
    copies = [
        pltpu.make_async_copy(loaded_any, loaded_ref, sems.at[0]),
        pltpu.make_async_copy(tiles_any, tiles_ref, sems.at[1]),
    ]
    for copy in copies:
        copy.start()
    for copy in copies:
        copy.wait()
    wide = row_len // groups_seq
    step = 2 * row_len // LANES
    frame = lax.axis_index("seq")
    lane = iota((TILES, LANES), 1)
    which = iota((TILES, LANES), 0)
    label = jnp.zeros((TILES, LANES), F32)
    for tile in range(TILES):
        label = jnp.where(which == tile, tiles_ref[0, tile].astype(F32), label)
    for s in range(groups_seq):
        windows = []
        for r in range(2):
            block, off = divmod(r * row_len + wide * s - 2, LANES)
            first = jnp.zeros((TILES, LANES), F32)
            second = first
            if block >= 0:
                first = loaded_ref[:, 0, block * LANES : (block + 1) * LANES]
            if block + 1 < step:
                second = loaded_ref[:, 0, (block + 1) * LANES : (block + 2) * LANES]
            window = jnp.where(lane >= off, first, second)
            if off:
                window = pltpu.roll(window, LANES - off, 1)
            column = lane + (wide * s - 2)
            inside = (column >= 0) & (column < row_len) & (lane < wide + 4)
            window = jnp.where(inside, window, 0.0)
            window = jnp.where(lane == wide + 4, label, window)
            place = (2 * frame + r).astype(F32)
            windows.append(jnp.where(lane == wide + 5, place, window))
        for j in range(3):
            rows = [window[t : t + 1] for window in windows for t in (j, j + 3)]
            rows = jnp.concatenate(rows, 0)
            for i in range(groups_dp):
                out_ref[i * groups_seq + s, :, j * LANES : (j + 1) * LANES] = rows


def prep_kernel(
    clips, wide, bucket_ref, in_weight_ref, in_bias_ref, bucket_bias_ref, norm_gain_ref, mid_weight_ref, mid_bias_ref,
    head_gain_ref, head_weight_ref, head_bias_ref, entry_ref, mid_ref, mend_ref, head_ref, cols_ref, fold_ref,
):
    ch = norm_gain_ref.shape[1]
    zch = head_bias_ref.shape[1]
    lane_pad = jnp.zeros((1, LANES - ch), F32)
    rows = [0.5 * norm_gain_ref[...], mid_bias_ref[...], 0.5 * head_gain_ref[...]]
    for clip in range(clips):
        rows.append(in_bias_ref[...] + bucket_bias_ref[pl.ds(bucket_ref[clip], 1), :])
    rows = [jnp.concatenate([row, lane_pad], 1) for row in rows]
    rows.append(jnp.zeros((LANES - len(rows), LANES), F32))
    table = jnp.concatenate(rows, 0).T
    for n in range(3):
        cols_ref[n] = jnp.broadcast_to(table[:ch, n : n + 1], (ch, LANES))
    spots = iota((ch, 2 * LANES), 1)
    offsets = jnp.zeros((ch, 2 * LANES), F32)
    for clip in range(clips):
        offsets = jnp.where(spots == 72 + clip, table[:ch, 3 + clip : 4 + clip], offsets)

    w_high, w_low = halves(in_weight_ref[...])
    taps = in_weight_ref.shape[0]
    tap = iota((taps, 2 * LANES), 0)
    place = iota((taps, 2 * LANES), 1)
    back = jnp.where(place >= SLOT, 1, 0) + jnp.where(place >= 2 * SLOT, 1, 0)
    inner = place - back * SLOT
    step_col = jnp.where(inner >= 24, 1, 0) + jnp.where(inner >= 48, 1, 0)
    colour = (inner - 24 * step_col) >> 3
    frame_row = inner & 7
    used = (place < 3 * SLOT) & (inner < 72)
    for h in range(6):
        step_row = frame_row - h
        wanted = 27 * (2 - back) + 9 * step_row + 3 * step_col + colour
        hot = used & (step_row >= 0) & (step_row < 3) & (tap == wanted)
        hot = jnp.where(hot, 1.0, 0.0).astype(BF16)
        off_high, off_low = halves(offsets)
        high = (mm_tn(w_high, hot) + off_high.astype(F32)).astype(BF16)
        low = (mm_tn(w_low, hot) + off_low.astype(F32)).astype(BF16)
        entry_ref[h * ch : (h + 1) * ch, :] = jnp.concatenate([high, low, high], 1)

    for d in range(3):
        blocks, mends = [], []
        for back in range(3):
            taps = [mid_weight_ref[9 * (2 - back) + 3 * b + d] for b in range(3)]
            exact = jnp.concatenate(taps, 1)
            high = exact.astype(BF16)
            blocks += [high, high[:, :MOVED]]
            mends += [(exact - high.astype(F32)) * 2.0**20, exact[:, MOVED:] * 2.0**11]
        for ref, parts, dtype in ((mid_ref, blocks, BF16), (mend_ref, mends, F8)):
            depth = sum(part.shape[1] for part in parts)
            if depth < ref.shape[1]:
                parts.append(jnp.zeros((ch, ref.shape[1] - depth), parts[0].dtype))
            ref[d * ch : (d + 1) * ch, :] = jnp.concatenate(parts, 1).astype(dtype)

    row = iota((LANES, zch), 0)
    channel = (row >> 2) & (zch - 1)
    pick = jnp.where(channel == iota((LANES, zch), 1), 1.0, 0.0)
    high, low = halves(head_weight_ref[...])
    parity = (iota((LANES, ch), 0) >> 1) & 1
    parts = []
    for weight in (high, low):
        spread = mm(pick.astype(BF16), weight)
        parts.append(jnp.concatenate([jnp.where(parity == r, spread, 0.0) for r in range(2)], 1))
    bias = jnp.sum(pick * head_bias_ref[...], axis=1, keepdims=True)
    bias_high, bias_low = halves(jnp.broadcast_to(bias, (LANES, 64)))
    spot = iota((LANES, 64), 1)
    tail = jnp.where(spot == 0, bias_high.astype(F32), jnp.where(spot == 1, bias_low.astype(F32), 0.0))
    head_ref[...] = jnp.concatenate([parts[0], parts[1], parts[0], tail], 1).astype(BF16)

    out = iota(fold_ref.shape, 0)
    src = iota(fold_ref.shape, 1)
    lane = src & (LANES - 1)
    hit = (((src >> 7) & 1) == (out & 1)) & (lane >= 2) & (lane < wide + 2) & (((lane - 2) >> 2) == (out >> 1))
    fold_ref[...] = jnp.where(hit, 1.0, 0.0).astype(BF16)


def main_kernel(
    clips, groups_dp, row_len, recv_ref, entry_ref, mid_ref, mend_ref, head_ref, cols_ref, fold_ref, out_any,
    pixels, q_high, q_low, s_high, s_mend, kept, tokens_ref, sems,
):
    frames_all = clips * FRAMES
    wide = out_any.shape[2] // 32
    ch = kept.shape[1]
    deep, deep_mend = 3 * ch + MOVED, 6 * ch - MOVED
    band = lax.axis_index("dp")
    column_band = lax.axis_index("seq")

    cells = [recv_ref[:, k, j * LANES : (j + 1) * LANES] for k in range(4) for j in range(3)]
    high, low = halves(jnp.concatenate(cells, 0))
    picks = iota((16, LANES), 0)
    picks = iota((16, LANES), 1) == jnp.where(picks < 8, wide + 4, wide + 5)
    tags = lax.dot_general(jnp.where(picks, 1.0, 0.0).astype(BF16), high, NT, preferred_element_type=F32)
    label, place = tags[:8], tags[8:]
    row = iota(label.shape, 0)
    pair = (band * 4 - 2 + row) >> 1
    first = ((pair >> 1) * TILES + (pair & 1)).astype(F32)
    of_colour = [label == first + 2.0 * c for c in range(3)]
    blocks = []
    for g in range(frames_all):
        here = place == (2 * g + (row & 1)).astype(F32)
        blocks += [jnp.where(here & hit, 1.0, 0.0) for hit in of_colour]
    order = jnp.concatenate(blocks, 0).astype(BF16)
    pixels[...] = mm(order, jnp.concatenate([high, low], 1))

    early = pl.ds(FRAMES * SLOT, q_high.shape[1] - FRAMES * SLOT)
    for ref in (q_high, q_low):
        for n in range(ref.shape[0]):
            ref[n, early, :] = jnp.zeros((early.size, LANES), BF16)

    lane = iota((1, LANES), 1)
    column = lane + (wide * column_band - 2)
    inside = jnp.where((column >= 0) & (column < row_len), 1.0, 0.0)
    masks = [inside] * 6
    masks[0] = jnp.where(band > 0, inside, 0.0)
    masks[5] = jnp.where(band < groups_dp - 1, inside, 0.0)
    ones = jnp.where(iota((64, 2 * LANES), 0) < 2, 1.0, 0.0).astype(BF16)
    phase = iota((LANES, 2 * LANES), 0)
    phase = ((phase >> 6) << 1) + (phase & 1)
    on_phase = ((iota((LANES, 2 * LANES), 1) - 2) & 3) == phase

    def active(values, half_gain, mask):
        square = jnp.sum(values * values, axis=0, keepdims=True) * (1.0 / ch)
        scale = lax.rsqrt(square + EPSILON)
        if mask is not None:
            scale = scale * mask
        half = values * scale * half_gain
        return half + half * jnp.tanh(half)

    def gather(clip):
        side = clip % 2
        for f in range(FRAMES):
            rows = pixels[(clip * FRAMES + f) * 24 : (clip * FRAMES + f + 1) * 24, :]
            for part, ref in ((0, q_high), (1, q_low)):
                cells = rows[:, part * LANES : (part + 1) * LANES]
                spare = jnp.where(iota((8, LANES), 0) == (-1 if part else clip), 1.0, 0.0)
                stack = [pltpu.roll(cells, 1, 1), cells, pltpu.roll(cells, LANES - 1, 1), spare]
                ref[side, (FRAMES - 1 - f) * SLOT : (FRAMES - f) * SLOT, :] = jnp.concatenate(stack, 0).astype(BF16)

    def enter(clip, f):
        side = clip % 2
        at = [(FRAMES - 1 - f - k) * SLOT for k in range(2)]
        right = [jnp.concatenate([ref[side, p : p + 2 * LANES, :] for p in at], 1) for ref in (q_high, q_low)]
        entry = mm(entry_ref[...], jnp.concatenate([right[0], right[0], right[1]], 0))
        for k in range(2):
            base = FRAMES - 1 - f - k
            for h in range(6):
                cell = entry[h * ch : (h + 1) * ch, k * LANES : (k + 1) * LANES]
                if 1 <= h <= 4:
                    kept[side * FRAMES + f + k, :, (h - 1) * LANES : h * LANES] = cell + cols_ref[1]
                act = active(cell, cols_ref[0], masks[h])
                act_high = act.astype(BF16)
                rest = act - act_high.astype(F32)
                low = rest[:MOVED].astype(BF16)
                rest = (rest * 2.0**13).astype(F8)
                coarse = (act * 2.0**4).astype(F8)
                for b in range(3):
                    if 0 <= h - b < 4:
                        lanes = pl.ds((h - b) * LANES, LANES)
                        at = base * deep + b * ch
                        s_high[side, at : at + ch, lanes] = act_high
                        at = base * deep_mend + b * ch
                        s_mend[side, at : at + ch, lanes] = coarse
                        at += 3 * ch - MOVED
                        if b:
                            s_mend[side, at : at + ch, lanes] = rest
                        else:
                            s_mend[side, at + MOVED : at + ch, lanes] = rest[MOVED:]
                            at = base * deep + 3 * ch
                            s_high[side, at : at + MOVED, lanes] = low

    def finish(clip, f):
        side = clip % 2
        def conv(weights, stack, per_frame):
            depth = per_frame * min(f + 1, 3)
            start = (FRAMES - 1 - f) * per_frame
            right = stack[side, start : start + depth, :]
            if depth % LANES:
                right = jnp.concatenate([right, jnp.zeros((-depth % LANES, 4 * LANES), stack.dtype)], 0)
            return mm(weights[:, : right.shape[0]], right)

        total = conv(mid_ref, s_high, deep) + conv(mend_ref, s_mend, deep_mend) * 2.0**-24
        acts = []
        for h in range(4):
            cell = total[:, h * LANES : (h + 1) * LANES]
            mixed = kept[side * FRAMES + f, :, h * LANES : (h + 1) * LANES] + cell[ch : 2 * ch]
            mixed = mixed + pltpu.roll(cell[:ch], 1, 1) + pltpu.roll(cell[2 * ch :], LANES - 1, 1)
            acts.append(active(mixed, cols_ref[2], None))
        top = jnp.concatenate([acts[0], acts[2]], 1)
        bottom = jnp.concatenate([acts[1], acts[3]], 1)
        act_high, act_low = halves(jnp.concatenate([top, bottom], 0))
        latent = mm(head_ref[...], jnp.concatenate([act_high, act_high, act_low, ones], 0))
        lat_high, lat_low = halves(jnp.where(on_phase, latent, 0.0))
        tokens = lax.dot_general(
            fold_ref[...], jnp.concatenate([lat_high, lat_low], 1), NT, preferred_element_type=F32
        )
        g = clip * FRAMES + f
        for n in range(wide // 4):
            tokens_ref[g, :, n * LANES : (n + 1) * LANES] = tokens[2 * n : 2 * n + 2]
        pltpu.make_async_copy(tokens_ref.at[g], out_any.at[g], sems.at[g]).start()

    gather(0)
    enter(0, 0)
    enter(0, 2)
    for clip in range(clips):
        later = clip + 1 < clips
        finish(clip, 0)
        if later:
            gather(clip + 1)
            enter(clip + 1, 0)
        finish(clip, 1)
        finish(clip, 2)
        if later:
            enter(clip + 1, 2)
        finish(clip, 3)
    for g in range(frames_all):
        pltpu.make_async_copy(tokens_ref.at[g], out_any.at[g], sems.at[g]).wait()


def body(
    loaded, tile_rows, bucket_ids, in_weight, in_bias, bucket_bias, norm_gain, mid_weight, mid_bias, head_gain,
    head_weight, head_bias,
):
    groups_dp = lax.axis_size("dp")
    groups_seq = lax.axis_size("seq")
    row_len = loaded.shape[2] // 2
    wide = row_len // groups_seq
    clips = bucket_ids.shape[0]
    frames_all = clips * FRAMES
    ch = norm_gain.shape[0]
    devices = groups_dp * groups_seq
    deep, deep_mend = 3 * ch + MOVED, 6 * ch - MOVED
    vmem = pl.BlockSpec(memory_space=pltpu.VMEM)
    place = pl.BlockSpec(memory_space=pl.ANY)
    part = pltpu.CompilerParams(vmem_limit_bytes=40 * 1024 * 1024)
    whole = pltpu.CompilerParams(vmem_limit_bytes=60 * 1024 * 1024)

    message = pl.pallas_call(
        functools.partial(send_kernel, groups_dp, groups_seq, row_len),
        out_shape=jax.ShapeDtypeStruct((devices, 4, 3 * LANES), F32),
        in_specs=[place] * 2,
        out_specs=vmem,
        scratch_shapes=[
            pltpu.VMEM((TILES, 1, 2 * row_len), F32),
            pltpu.SMEM((1, TILES), jnp.int32),
            pltpu.SemaphoreType.DMA((2,)),
        ],
        compiler_params=whole,
        name="send_windows",
    )(loaded.transpose(1, 0, 2), tile_rows)
    arrived = lax.all_to_all(message, ("dp", "seq"), split_axis=0, concat_axis=0, tiled=True)

    fold_rows = -(-(wide // 2) // 16) * 16
    operands = (
        bucket_ids, in_weight.T, in_bias[None], bucket_bias, norm_gain[None], mid_weight, mid_bias[None],
        head_gain[None], head_weight, head_bias[None],
    )
    weights = pl.pallas_call(
        functools.partial(prep_kernel, clips, wide),
        out_shape=(
            jax.ShapeDtypeStruct((6 * ch, 6 * LANES), BF16),
            jax.ShapeDtypeStruct((3 * ch, -(-3 * deep // LANES) * LANES), BF16),
            jax.ShapeDtypeStruct((3 * ch, -(-3 * deep_mend // LANES) * LANES), F8),
            jax.ShapeDtypeStruct((LANES, 6 * ch + 64), BF16),
            jax.ShapeDtypeStruct((3, ch, LANES), F32),
            jax.ShapeDtypeStruct((fold_rows, 4 * LANES), BF16),
        ),
        in_specs=[pl.BlockSpec(memory_space=pltpu.SMEM)] + [vmem] * (len(operands) - 1),
        out_specs=(vmem,) * 6,
        compiler_params=part,
        name="prepare_weights",
    )(*operands)
    sides = min(clips, 2)
    return pl.pallas_call(
        functools.partial(main_kernel, clips, groups_dp, row_len),
        out_shape=jax.ShapeDtypeStruct((frames_all, 2, wide * 32), F32),
        in_specs=[vmem] * 7,
        out_specs=place,
        scratch_shapes=[
            pltpu.VMEM((frames_all * 24, 2 * LANES), F32),
            pltpu.VMEM((sides, (FRAMES + 2) * SLOT + 16, LANES), BF16),
            pltpu.VMEM((sides, (FRAMES + 2) * SLOT + 16, LANES), BF16),
            pltpu.VMEM((sides, FRAMES * deep, 4 * LANES), BF16),
            pltpu.VMEM((sides, FRAMES * deep_mend, 4 * LANES), F8),
            pltpu.VMEM((sides * FRAMES, ch, 4 * LANES), F32),
            pltpu.VMEM((frames_all, 2, wide * 32), F32),
            pltpu.SemaphoreType.DMA((frames_all,)),
        ],
        compiler_params=part,
        name="encode_columns",
    )(arrived, *weights)


def solution(mesh):
    return jax.shard_map(
        body,
        mesh=mesh,
        in_specs=(P("seq", "dp", None), P("seq", "dp")) + (P(),) * 10,
        out_specs=P(None, "dp", "seq"),
        check_vma=False,
    )
```

```python
import functools

import jax
import jax.numpy as jnp
from jax import lax
from jax.experimental import pallas as pl
from jax.experimental.pallas import tpu as pltpu
from jax.sharding import PartitionSpec as P

FRAMES = 4
EPSILON = 1e-06
LANES = 128
TILES = 6
SLOT = 48
BAND = 3 * SLOT
BF16 = jnp.bfloat16
F32 = jnp.float32
F8 = jnp.float8_e4m3fn
NT = (((1,), (1,)), ((), ()))
TN = (((0,), (0,)), ((), ()))


def iota(shape, dim):
    return lax.broadcasted_iota(jnp.int32, shape, dim)


def halves(values):
    high = values.astype(BF16)
    return high, (values - high.astype(F32)).astype(BF16)


def mm(a, b):
    return jnp.dot(a, b, preferred_element_type=F32)


def mm_tn(a, b):
    return lax.dot_general(a, b, TN, preferred_element_type=F32)


def split_row(row):
    frame_row = sum(jnp.where(row >= 3 * n, 1, 0) for n in range(1, 8))
    return frame_row, row - 3 * frame_row


def send_kernel(groups_dp, groups_seq, row_len, loaded_any, tiles_any, out_ref, loaded_ref, tiles_ref, sems):
    copies = [
        pltpu.make_async_copy(loaded_any, loaded_ref, sems.at[0]),
        pltpu.make_async_copy(tiles_any, tiles_ref, sems.at[1]),
    ]
    for copy in copies:
        copy.start()
    for copy in copies:
        copy.wait()
    wide = row_len // groups_seq
    step = 2 * row_len // LANES
    frame = lax.axis_index("seq")
    lane = iota((TILES, LANES), 1)
    which = iota((TILES, LANES), 0)
    label = jnp.zeros((TILES, LANES), F32)
    for tile in range(TILES):
        label = jnp.where(which == tile, tiles_ref[0, tile].astype(F32), label)
    for s in range(groups_seq):
        windows = []
        for r in range(2):
            block, off = divmod(r * row_len + wide * s - 2, LANES)
            first = jnp.zeros((TILES, LANES), F32)
            second = first
            if block >= 0:
                first = loaded_ref[:, 0, block * LANES : (block + 1) * LANES]
            if block + 1 < step:
                second = loaded_ref[:, 0, (block + 1) * LANES : (block + 2) * LANES]
            window = jnp.where(lane >= off, first, second)
            if off:
                window = pltpu.roll(window, LANES - off, 1)
            column = lane + (wide * s - 2)
            inside = (column >= 0) & (column < row_len) & (lane < wide + 4)
            window = jnp.where(inside, window, 0.0)
            window = jnp.where(lane == wide + 4, label, window)
            place = (2 * frame + r).astype(F32)
            windows.append(jnp.where(lane == wide + 5, place, window))
        for j in range(3):
            rows = [window[t : t + 1] for window in windows for t in (j, j + 3)]
            rows = jnp.concatenate(rows, 0)
            for i in range(groups_dp):
                out_ref[i * groups_seq + s, :, j * LANES : (j + 1) * LANES] = rows


def collect_kernel(clips, *refs):
    sources, out_ref, held, sems = refs[:8], refs[8], refs[9:17], refs[17]
    copies = [pltpu.make_async_copy(src, dst, sems.at[n]) for n, (src, dst) in enumerate(zip(sources, held))]
    for copy in copies:
        copy.start()
    out_ref[...] = jnp.zeros(out_ref.shape, F32)
    for copy in copies:
        copy.wait()
    bucket, in_bias, bucket_bias, norm_gain, mid_bias, head_gain, head_weight, head_bias = held
    ch = norm_gain.shape[1]
    out_ref[0:1, :ch] = 0.5 * norm_gain[...]
    out_ref[1:2, :ch] = mid_bias[...]
    out_ref[2:3, :ch] = 0.5 * head_gain[...]
    for clip in range(clips):
        out_ref[3 + clip : 4 + clip, :ch] = in_bias[...] + bucket_bias[pl.ds(bucket[clip], 1), :]
    out_ref[8:9, : head_bias.shape[1]] = head_bias[...]
    out_ref[16:, :ch] = head_weight[...]


def prep_kernel(
    clips, wide, vectors_ref, in_weight_ref, mid_weight_ref, entry_ref, mid_ref, mend_ref, head_ref, cols_ref, fold_ref
):
    ch = cols_ref.shape[1]
    zch = vectors_ref.shape[0] - 16
    rows = [vectors_ref[...], jnp.zeros((LANES - vectors_ref.shape[0], LANES), F32)]
    table = jnp.concatenate(rows, 0).T
    for n in range(3):
        cols_ref[n] = jnp.broadcast_to(table[:ch, n : n + 1], (ch, LANES))
    spots = iota((ch, 4 * LANES - 3 * BAND), 1)
    offsets = jnp.zeros(spots.shape, F32)
    for clip in range(clips):
        exact = jnp.broadcast_to(table[:ch, 3 + clip : 4 + clip], spots.shape)
        off_high, off_low = halves(exact)
        offsets = jnp.where(spots == 2 * clip, off_high.astype(F32), offsets)
        offsets = jnp.where(spots == 2 * clip + 1, off_low.astype(F32), offsets)
    offsets = offsets.astype(BF16)

    w_high, w_low = halves(in_weight_ref[...])
    taps = in_weight_ref.shape[0]
    tap = iota((taps, 2 * LANES), 0)
    place = iota((taps, 2 * LANES), 1)
    back = jnp.where(place >= SLOT, 1, 0) + jnp.where(place >= 2 * SLOT, 1, 0)
    step_col = ((place - back * SLOT) >> 4) & 3
    for group in range(2):
        frame_row, colour = split_row((place & 15) + 8 * group)
        for k in range(3):
            step_row = frame_row - (3 * group + k)
            wanted = 27 * (2 - back) + 9 * step_row + 3 * step_col + colour
            hot = (place < BAND) & (step_row >= 0) & (step_row < 3) & (tap == wanted)
            hot = jnp.where(hot, 1.0, 0.0).astype(BF16)
            high = mm_tn(w_high, hot).astype(BF16)[:, :BAND]
            low = mm_tn(w_low, hot).astype(BF16)[:, :BAND]
            entry_ref[group, k * ch : (k + 1) * ch, :] = jnp.concatenate([high, low, high, offsets], 1)

    for d in range(3):
        blocks, mends = [], []
        for back in range(3):
            taps = [mid_weight_ref[9 * (2 - back) + 3 * b + d] for b in range(3)]
            exact = jnp.concatenate(taps, 1)
            high = exact.astype(BF16)
            blocks.append(high)
            mends += [(exact - high.astype(F32)) * 2.0**20, exact * 2.0**11]
        for ref, parts, dtype in ((mid_ref, blocks, BF16), (mend_ref, mends, F8)):
            depth = sum(part.shape[1] for part in parts)
            if depth < ref.shape[1]:
                parts.append(jnp.zeros((ch, ref.shape[1] - depth), parts[0].dtype))
            ref[d * ch : (d + 1) * ch, :] = jnp.concatenate(parts, 1).astype(dtype)

    row = iota((LANES, zch), 0)
    channel = (row >> 2) & (zch - 1)
    pick = jnp.where(channel == iota((LANES, zch), 1), 1.0, 0.0)
    high, low = halves(vectors_ref[16:, :ch])
    parity = (iota((LANES, ch), 0) >> 1) & 1
    parts = []
    for weight in (high, low):
        spread = mm(pick.astype(BF16), weight)
        parts.append(jnp.concatenate([jnp.where(parity == r, spread, 0.0) for r in range(2)], 1))
    bias = jnp.sum(pick * vectors_ref[8:9, :zch], axis=1, keepdims=True)
    bias_high, bias_low = halves(jnp.broadcast_to(bias, (LANES, 64)))
    spot = iota((LANES, 64), 1)
    tail = jnp.where(spot == 0, bias_high.astype(F32), jnp.where(spot == 1, bias_low.astype(F32), 0.0))
    head_ref[...] = jnp.concatenate([parts[0], parts[1], parts[0], tail], 1).astype(BF16)

    out = iota(fold_ref.shape, 0)
    src = iota(fold_ref.shape, 1)
    lane = src & (LANES - 1)
    hit = (((src >> 7) & 1) == (out & 1)) & (lane >= 2) & (lane < wide + 2) & (((lane - 2) >> 2) == (out >> 1))
    fold_ref[...] = jnp.where(hit, 1.0, 0.0).astype(BF16)


def main_kernel(
    clips, groups_dp, row_len, recv_ref, entry_ref, mid_ref, mend_ref, head_ref, cols_ref, fold_ref, out_any,
    pixels, q_high, q_low, s_high, s_mend, kept, entered, total, last, tokens_ref, sems,
):
    frames_all = clips * FRAMES
    wide = out_any.shape[2] // 32
    ch = kept.shape[1]
    band = lax.axis_index("dp")
    column_band = lax.axis_index("seq")

    cells = [recv_ref[:, k, j * LANES : (j + 1) * LANES] for k in range(4) for j in range(3)]
    high, low = halves(jnp.concatenate(cells, 0))
    picks = iota((16, LANES), 0)
    picks = iota((16, LANES), 1) == jnp.where(picks < 8, wide + 4, wide + 5)
    tags = lax.dot_general(jnp.where(picks, 1.0, 0.0).astype(BF16), high, NT, preferred_element_type=F32)
    label, place = tags[:8], tags[8:]
    hits, sides = [], []
    for third in range(3):
        frame_row, colour = split_row(iota(label.shape, 0) + 8 * third)
        pair = (band * 4 - 2 + frame_row) >> 1
        hits.append(label == ((pair >> 1) * TILES + (pair & 1) + 2 * colour).astype(F32))
        sides.append((frame_row & 1).astype(F32))
    blocks = []
    for g in range(frames_all):
        for hit, half in zip(hits, sides):
            blocks.append(jnp.where(hit & (place == half + 2.0 * g), 1.0, 0.0))
    order = jnp.concatenate(blocks, 0).astype(BF16)
    pixels[...] = mm(order, jnp.concatenate([high, low], 1))

    for ref in (q_high, q_low):
        for n in range(ref.shape[0]):
            for group in range(2):
                ref[n, group, FRAMES * SLOT :, :] = jnp.zeros((2 * SLOT, LANES), BF16)

    lane = iota((1, LANES), 1)
    column = lane + (wide * column_band - 2)
    inside = jnp.where((column >= 0) & (column < row_len), 1.0, 0.0)
    masks = [inside] * 6
    masks[0] = jnp.where(band > 0, inside, 0.0)
    masks[5] = jnp.where(band < groups_dp - 1, inside, 0.0)
    ones = jnp.where(iota((64, 2 * LANES), 0) < 2, 1.0, 0.0).astype(BF16)
    phase = iota((LANES, 2 * LANES), 0)
    phase = ((phase >> 6) << 1) + (phase & 1)
    on_phase = ((iota((LANES, 2 * LANES), 1) - 2) & 3) == phase

    def active(values, half_gain, mask):
        square = jnp.sum(values * values, axis=0, keepdims=True) * (1.0 / ch)
        scale = lax.rsqrt(square + EPSILON)
        if mask is not None:
            scale = scale * mask
        half = values * scale * half_gain
        return half + half * jnp.tanh(half)

    def gather(clip):
        side = clip % 2
        for f in range(FRAMES):
            rows = pixels[(clip * FRAMES + f) * 24 : (clip * FRAMES + f + 1) * 24, :]
            for part, ref in ((0, q_high), (1, q_low)):
                cells = rows[:, part * LANES : (part + 1) * LANES]
                stack = [pltpu.roll(cells, 1, 1), cells, pltpu.roll(cells, LANES - 1, 1)]
                at = (FRAMES - 1 - f) * SLOT
                for group in range(2):
                    rows_in = jnp.concatenate([step[8 * group : 8 * group + 16] for step in stack], 0)
                    ref[side, group, at : at + SLOT, :] = rows_in.astype(BF16)

    def enter(g, group):
        clip, f = divmod(g, FRAMES)
        at = [(FRAMES - 1 - f - k) * SLOT for k in range(2)]
        high, low = [
            jnp.concatenate([ref[clip % 2, group, p : p + BAND, :] for p in at], 1) for ref in (q_high, q_low)
        ]
        spare = iota((4 * LANES - 3 * BAND, 2 * LANES), 0) >> 1
        spare = jnp.where(spare == clip, 1.0, 0.0).astype(BF16)
        entered[group] = mm(entry_ref[group], jnp.concatenate([high, high, low, spare], 0))

    def activate(g, rows):
        clip, f = divmod(g, FRAMES)
        side, base, k = clip % 2, FRAMES - 1 - f, f % 2
        for h in rows:
            cell = entered[h // 3, h % 3 * ch : (h % 3 + 1) * ch, k * LANES : (k + 1) * LANES]
            if 1 <= h <= 4:
                kept[side * FRAMES + f, :, (h - 1) * LANES : h * LANES] = cell + cols_ref[1]
            act = active(cell, cols_ref[0], masks[h])
            act_high = act.astype(BF16)
            rest = ((act - act_high.astype(F32)) * 2.0**13).astype(F8)
            coarse = (act * 2.0**4).astype(F8)
            for b in range(3):
                if 0 <= h - b < 4:
                    lanes = pl.ds((h - b) * LANES, LANES)
                    s_high[side, pl.ds((3 * base + b) * ch, ch), lanes] = act_high
                    s_mend[side, pl.ds((6 * base + b) * ch, ch), lanes] = coarse
                    s_mend[side, pl.ds((6 * base + 3 + b) * ch, ch), lanes] = rest

    def convolve(g, p):
        clip, f = divmod(g, FRAMES)

        def conv(weights, stack, per_frame):
            depth = per_frame * min(f + 1, 3)
            start = (FRAMES - 1 - f) * per_frame
            right = stack[clip % 2, start : start + depth, 2 * p * LANES : 2 * (p + 1) * LANES]
            if depth % LANES:
                right = jnp.concatenate([right, jnp.zeros((-depth % LANES, 2 * LANES), stack.dtype)], 0)
            return mm(weights[:, : right.shape[0]], right)

        total[p] = conv(mid_ref, s_high, 3 * ch) + conv(mend_ref, s_mend, 6 * ch) * 2.0**-24

    def settle(g, p):
        clip, f = divmod(g, FRAMES)
        for r in range(2):
            h = 2 * p + r
            cell = total[p, :, r * LANES : (r + 1) * LANES]
            mixed = kept[clip % 2 * FRAMES + f, :, h * LANES : (h + 1) * LANES] + cell[ch : 2 * ch]
            mixed = mixed + pltpu.roll(cell[:ch], 1, 1) + pltpu.roll(cell[2 * ch :], LANES - 1, 1)
            act_high, act_low = halves(active(mixed, cols_ref[2], None))
            for part, act in enumerate((act_high, act_high, act_low)):
                at = (2 * part + r) * ch
                last[at : at + ch, p * LANES : (p + 1) * LANES] = act

    def finish(g):
        latent = mm(head_ref[...], last[...])
        lat_high, lat_low = halves(jnp.where(on_phase, latent, 0.0))
        tokens = lax.dot_general(
            fold_ref[...], jnp.concatenate([lat_high, lat_low], 1), NT, preferred_element_type=F32
        )
        for n in range(wide // 4):
            tokens_ref[g, :, n * LANES : (n + 1) * LANES] = tokens[2 * n : 2 * n + 2]
        pltpu.make_async_copy(tokens_ref.at[g], out_any.at[g], sems.at[g]).start()

    last[6 * ch :, :] = ones
    gather(0)
    enter(0, 0)
    enter(0, 1)
    activate(0, range(6))
    for g in range(frames_all):
        after = g + 1
        more = after < frames_all
        if more and after % FRAMES == 0:
            gather(after // FRAMES)
        if more and after % 2 == 0:
            enter(after, 0)
        convolve(g, 0)
        if more and after % 2 == 0:
            enter(after, 1)
        if more:
            activate(after, range(3))
        if g:
            settle(g - 1, 1)
            finish(g - 1)
        convolve(g, 1)
        if more:
            activate(after, range(3, 6))
        settle(g, 0)
    settle(frames_all - 1, 1)
    finish(frames_all - 1)
    for g in range(frames_all):
        pltpu.make_async_copy(tokens_ref.at[g], out_any.at[g], sems.at[g]).wait()


def body(
    loaded, tile_rows, bucket_ids, in_weight, in_bias, bucket_bias, norm_gain, mid_weight, mid_bias, head_gain,
    head_weight, head_bias,
):
    groups_dp = lax.axis_size("dp")
    groups_seq = lax.axis_size("seq")
    row_len = loaded.shape[2] // 2
    wide = row_len // groups_seq
    clips = bucket_ids.shape[0]
    frames_all = clips * FRAMES
    ch = norm_gain.shape[0]
    devices = groups_dp * groups_seq
    deep, deep_mend = 3 * ch, 6 * ch
    vmem = pl.BlockSpec(memory_space=pltpu.VMEM)
    place = pl.BlockSpec(memory_space=pl.ANY)
    part = pltpu.CompilerParams(vmem_limit_bytes=40 * 1024 * 1024)
    whole = pltpu.CompilerParams(vmem_limit_bytes=60 * 1024 * 1024)

    message = pl.pallas_call(
        functools.partial(send_kernel, groups_dp, groups_seq, row_len),
        out_shape=jax.ShapeDtypeStruct((devices, 4, 3 * LANES), F32),
        in_specs=[place] * 2,
        out_specs=vmem,
        scratch_shapes=[
            pltpu.VMEM((TILES, 1, 2 * row_len), F32),
            pltpu.SMEM((1, TILES), jnp.int32),
            pltpu.SemaphoreType.DMA((2,)),
        ],
        compiler_params=whole,
        name="send_windows",
    )(loaded.transpose(1, 0, 2), tile_rows)
    message, bucket_ids = lax.optimization_barrier((message, bucket_ids))
    arrived = lax.all_to_all(message, ("dp", "seq"), split_axis=0, concat_axis=0, tiled=True)

    fold_rows = -(-(wide // 2) // 16) * 16
    zch = head_bias.shape[0]
    small = (
        bucket_ids, in_bias[None], bucket_bias, norm_gain[None], mid_bias[None], head_gain[None], head_weight,
        head_bias[None],
    )
    held = [pltpu.SMEM(bucket_ids.shape, jnp.int32)] + [pltpu.VMEM(op.shape, F32) for op in small[1:]]
    vectors = pl.pallas_call(
        functools.partial(collect_kernel, clips),
        out_shape=jax.ShapeDtypeStruct((16 + zch, LANES), F32),
        in_specs=[place] * len(small),
        out_specs=vmem,
        scratch_shapes=held + [pltpu.SemaphoreType.DMA((len(small),))],
        compiler_params=whole,
        name="collect_vectors",
    )(*small)
    weights = pl.pallas_call(
        functools.partial(prep_kernel, clips, wide),
        out_shape=(
            jax.ShapeDtypeStruct((2, 3 * ch, 4 * LANES), BF16),
            jax.ShapeDtypeStruct((3 * ch, -(-3 * deep // LANES) * LANES), BF16),
            jax.ShapeDtypeStruct((3 * ch, -(-3 * deep_mend // LANES) * LANES), F8),
            jax.ShapeDtypeStruct((LANES, 6 * ch + 64), BF16),
            jax.ShapeDtypeStruct((3, ch, LANES), F32),
            jax.ShapeDtypeStruct((fold_rows, 4 * LANES), BF16),
        ),
        in_specs=[vmem] * 3,
        out_specs=(vmem,) * 6,
        compiler_params=part,
        name="prepare_weights",
    )(vectors, in_weight.T, mid_weight)
    sides = min(clips, 2)
    return pl.pallas_call(
        functools.partial(main_kernel, clips, groups_dp, row_len),
        out_shape=jax.ShapeDtypeStruct((frames_all, 2, wide * 32), F32),
        in_specs=[vmem] * 7,
        out_specs=place,
        scratch_shapes=[
            pltpu.VMEM((frames_all * 24, 2 * LANES), F32),
            pltpu.VMEM((sides, 2, (FRAMES + 2) * SLOT, LANES), BF16),
            pltpu.VMEM((sides, 2, (FRAMES + 2) * SLOT, LANES), BF16),
            pltpu.VMEM((sides, FRAMES * deep, 4 * LANES), BF16),
            pltpu.VMEM((sides, FRAMES * deep_mend, 4 * LANES), F8),
            pltpu.VMEM((sides * FRAMES, ch, 4 * LANES), F32),
            pltpu.VMEM((2, 3 * ch, 2 * LANES), F32),
            pltpu.VMEM((2, 3 * ch, 2 * LANES), F32),
            pltpu.VMEM((6 * ch + 64, 2 * LANES), BF16),
            pltpu.VMEM((frames_all, 2, wide * 32), F32),
            pltpu.SemaphoreType.DMA((frames_all,)),
        ],
        compiler_params=part,
        name="encode_columns",
    )(arrived, *weights)


def solution(mesh):
    return jax.shard_map(
        body,
        mesh=mesh,
        in_specs=(P("seq", "dp", None), P("seq", "dp")) + (P(),) * 10,
        out_specs=P(None, "dp", "seq"),
        check_vma=False,
    )
```
